32 devices in a mesh: dp: 16 (over z, y, core), tp: 2 (over x).
Axes of the slice: x: 2, y: 2, z: 4, core: 2. Of those that a mesh axis runs over, the one named last changes fastest.
Arguments:
- tokens: bfloat16 [17408, 768], P('dp'), may hold values from -6 to 6
- latents: bfloat16 [17408, 1024], P('dp'), may hold values from -6 to 6
- grad_block: bfloat16 [17408, 768], P('dp'), may hold values from -6 to 6
- grad_head: bfloat16 [17408, 1024], P('dp'), may hold values from -6 to 6
- image_lengths: int32 [16, 3], P('dp'), may hold values from 0 to 1088, as said below
- ln1_gain: float32 [768], replicated, may hold values from 0.5 to 1.5
- ln1_bias: float32 [768], replicated, may hold values from -1.8 to 1.8
- w_qkv: bfloat16 [3, 768, 768], P(None, 'dp', 'tp'), may hold values from -0.21875 to 0.21875
- b_qv: float32 [2, 768], P(None, 'tp'), may hold values from -1.8 to 1.8
- w_out: bfloat16 [768, 768], P('dp', 'tp'), may hold values from -1.75 to 1.75
- b_out: float32 [768], replicated, may hold values from -1.8 to 1.8
- ln2_gain: float32 [768], replicated, may hold values from 0.5 to 1.5
- ln2_bias: float32 [768], replicated, may hold values from -1.8 to 1.8
- w_up: bfloat16 [768, 3072], P('dp', 'tp'), may hold values from -0.21875 to 0.21875
- b_up: float32 [3072], P('tp'), may hold values from -1.8 to 1.8
- w_down: bfloat16 [768, 3072], P('dp', 'tp'), may hold values from -0.109375 to 0.109375
- b_down: float32 [768], replicated, may hold values from -1.8 to 1.8
- w_mod: bfloat16 [3, 768, 1024], P(None, 'dp'), may hold values from -0.21875 to 0.21875
- b_mod: float32 [3, 1024], replicated, may hold values from -1.8 to 1.8
- w_hid1: bfloat16 [1024, 1024], P('dp', 'tp'), may hold values from -0.1875 to 0.1875
- b_hid1: float32 [1024], P('tp'), may hold values from -1.8 to 1.8
- w_hid2: bfloat16 [1024, 1024], P('dp', 'tp'), may hold values from -0.1875 to 0.1875
- b_hid2: float32 [1024], replicated, may hold values from -1.8 to 1.8
Outputs:
- block_out: bfloat16 [17408, 768], P('dp')
- head_out: bfloat16 [17408, 1024], P('dp')
- grad_tokens: float32 [17408, 768], P('dp')
- grad_latents: float32 [17408, 1024], P('dp')
- d_ln1_gain: float32 [768], replicated
- d_ln1_bias: float32 [768], replicated
- d_w_qkv: float32 [3, 768, 768], P(None, 'dp', 'tp')
- d_b_qv: float32 [2, 768], P(None, 'tp')
- d_w_out: float32 [768, 768], P('dp', 'tp')
- d_b_out: float32 [768], replicated
- d_ln2_gain: float32 [768], replicated
- d_ln2_bias: float32 [768], replicated
- d_w_up: float32 [768, 3072], P('dp', 'tp')
- d_b_up: float32 [3072], P('tp')
- d_w_down: float32 [768, 3072], P('dp', 'tp')
- d_b_down: float32 [768], replicated
- d_w_mod: float32 [3, 768, 1024], P(None, 'dp')
- d_b_mod: float32 [3, 1024], replicated
- d_w_hid1: float32 [1024, 1024], P('dp', 'tp')
- d_b_hid1: float32 [1024], P('tp')
- d_w_hid2: float32 [1024, 1024], P('dp', 'tp')
- d_b_hid2: float32 [1024], replicated
- rms_values: float32 [16, 4], P('dp')
The draws below stay inside these ranges and needn't reach their ends.
Inputs may be any that keep to these rules, and one draw needn't show every extreme that they name: `image_lengths`: each row describes one slot: either one image of 1088 tokens followed by two zeros, or three images of 320 tokens each, the slot's remaining rows being padding. Both kinds of row occur in every draw.
All inputs are finite; a program needn't handle non-finite values.
Results may differ from the reference program's by a relative error of at most 0.03.
Values may be sent and summed in bfloat16 or wider, within the bound.
No kernel may reach another device: no remote copies, remote signals or barrier semaphores. Data moves between devices by JAX's collectives and lax.ppermute only.
A program may use at most 256 MiB of HBM per device.

```python
import jax
import jax.numpy as jnp
from jax import lax

D = 768
HEADS = 12
HDIM = 64
FF = 3072
W = 1024
BUF = 64
LONG = 1024
SHORT = 256
SLOTS = 16
TOKENS = 17408
N_TP = 2


def draw_image_lengths(key, part):
    key = jax.random.fold_in(key, 7)
    kind_key, pick_key = jax.random.split(key)
    kinds = jax.random.randint(kind_key, (SLOTS,), 0, 2)
    picks = jax.random.permutation(pick_key, SLOTS)
    kinds = kinds.at[picks[0]].set(1).at[picks[1]].set(0)
    long_row = jnp.array([LONG + BUF, 0, 0], jnp.int32)
    short_row = jnp.full((3,), SHORT + BUF, jnp.int32)
    return jnp.where(kinds[:, None] == 1, long_row[None, :], short_row[None, :]).astype(jnp.int32)


def shard_levels(own_key, dims, shards, least, high):
    gain, own = 1.0, jax.random.fold_in(own_key, 6)
    for axis_at, shards_of in shards:
        heights = jnp.exp(jax.random.uniform(jax.random.fold_in(own, axis_at), (shards_of,), jnp.float32, least / len(shards), high / len(shards)))
        gain = gain * jnp.repeat(heights, dims[axis_at] // shards_of).reshape([-1 if axis == axis_at else 1 for axis in range(len(dims))])
    return gain


def noise(stream_key, shape, spread, limit, cuts=(), kind=jnp.bfloat16):
    values = jax.random.normal(stream_key, shape, jnp.float32) * spread
    if len(cuts) > 0:
        values = shard_levels(stream_key, shape, cuts, -0.22, 0.18) * values
    return jnp.clip(values, min=-limit, max=limit).astype(kind)


def setup_inputs(seed: int = 0) -> dict:
    arg_keys = jax.random.split(jax.random.key(seed), 24)
    tokens = noise(arg_keys[0], (TOKENS, D), 1.0, 6.0, ((0, 16),))
    latents = noise(arg_keys[1], (TOKENS, W), 1.0, 6.0, ((0, 16),))
    grad_block = noise(arg_keys[2], (TOKENS, D), 1.0, 6.0, ((0, 16),))
    grad_head = noise(arg_keys[3], (TOKENS, W), 1.0, 6.0, ((0, 16),))
    image_lengths = draw_image_lengths(jax.random.fold_in(arg_keys[23], 71), 0)
    ln1_gain = jnp.clip(1.0 + 0.1 * jax.random.normal(arg_keys[5], (D,), jnp.float32), 0.5, 1.5)
    ln1_bias = noise(arg_keys[6], (D,), 0.3, 1.8, (), jnp.float32)
    w_qkv = noise(arg_keys[7], (3, D, D), D ** -0.5, 0.21875, ((1, 16), (2, 2)))
    b_qv = noise(arg_keys[8], (2, D), 0.3, 1.8, ((1, 2),), jnp.float32)
    w_out = noise(arg_keys[9], (D, D), (D // 64) ** -0.5, 1.75, ((0, 16), (1, 2)))
    b_out = noise(arg_keys[10], (D,), 0.3, 1.8, (), jnp.float32)
    ln2_gain = jnp.clip(1.0 + 0.1 * jax.random.normal(arg_keys[11], (D,), jnp.float32), 0.5, 1.5)
    ln2_bias = noise(arg_keys[12], (D,), 0.3, 1.8, (), jnp.float32)
    w_up = noise(arg_keys[13], (D, FF), D ** -0.5, 0.21875, ((0, 16), (1, 2)))
    b_up = noise(arg_keys[14], (FF,), 0.3, 1.8, ((0, 2),), jnp.float32)
    w_down = noise(arg_keys[15], (D, FF), FF ** -0.5, 0.109375, ((0, 16), (1, 2)))
    b_down = noise(arg_keys[16], (D,), 0.3, 1.8, (), jnp.float32)
    w_mod = noise(arg_keys[17], (3, D, W), D ** -0.5, 0.21875, ((1, 16),))
    b_mod = noise(arg_keys[18], (3, W), 0.3, 1.8, (), jnp.float32)
    w_hid1 = noise(arg_keys[19], (W, W), W ** -0.5, 0.1875, ((0, 16), (1, 2)))
    b_hid1 = noise(arg_keys[20], (W,), 0.3, 1.8, ((0, 2),), jnp.float32)
    w_hid2 = noise(arg_keys[21], (W, W), W ** -0.5, 0.1875, ((0, 16), (1, 2)))
    b_hid2 = noise(arg_keys[22], (W,), 0.3, 1.8, (), jnp.float32)
    return dict(tokens=tokens, latents=latents, grad_block=grad_block, grad_head=grad_head, image_lengths=image_lengths, ln1_gain=ln1_gain, ln1_bias=ln1_bias, w_qkv=w_qkv, b_qv=b_qv, w_out=w_out, b_out=b_out, ln2_gain=ln2_gain, ln2_bias=ln2_bias, w_up=w_up, b_up=b_up, w_down=w_down, b_down=b_down, w_mod=w_mod, b_mod=b_mod, w_hid1=w_hid1, b_hid1=b_hid1, w_hid2=w_hid2, b_hid2=b_hid2)


EPS_NORM = 1e-06
HIGHEST = lax.Precision.HIGHEST

@jax.custom_vjp
def low(v):
    return lax.optimization_barrier(v.astype(jnp.bfloat16)).astype(jnp.float32)

@jax.custom_vjp
def low_back(v):
    return v

def low_keep(v):
    return (low(v), None)

def low_pass(kept, grad):
    return (grad,)

def back_keep(v):
    return (v, None)

def back_low(kept, grad):
    return (low(grad),)
low.defvjp(low_keep, low_pass)
low_back.defvjp(back_keep, back_low)

def layer_norm(values):
    row_mean = lax.optimization_barrier(jnp.mean(values, axis=-1, keepdims=True))
    centred = values - row_mean
    return centred * lax.rsqrt(lax.optimization_barrier(jnp.mean(centred * centred, axis=-1, keepdims=True)) + EPS_NORM)

def piece_bounds(total):
    piece_len = total // N_TP
    return [(piece_num * piece_len, (piece_num + 1) * piece_len) for piece_num in range(N_TP)]

def slot_masks(lengths):
    bounds = jnp.cumsum(lengths).astype(jnp.int32)
    positions = jnp.arange(LONG + BUF, dtype=jnp.int32)
    segment = lax.optimization_barrier(jnp.sum((positions[:, None] >= bounds[None, :]).astype(jnp.int32), axis=1)).astype(jnp.int32)
    starts = jnp.concatenate([jnp.zeros((1,), jnp.int32), bounds]).astype(jnp.int32)
    first_row = lax.optimization_barrier(jnp.sum(jnp.where(segment[:, None] == jnp.arange(4, dtype=jnp.int32)[None, :], starts[None, :], 0), axis=1)).astype(jnp.int32)
    valid_row = positions < bounds[2]
    image_row = valid_row & (positions - first_row >= BUF)
    return (segment, valid_row.astype(jnp.float32), image_row.astype(jnp.float32))

def slot_forward(tok_slot, lat_slot, params, segment, valid_row):
    ln1_gain, ln1_bias, w_qkv, b_qv, w_out, b_out, ln2_gain, ln2_bias, w_up, b_up, w_down, b_down, w_mod, b_mod, w_hid1, b_hid1, w_hid2, b_hid2 = params
    norm_one = low(layer_norm(tok_slot) * ln1_gain + ln1_bias)
    proj_all = jnp.concatenate([low_back(jnp.einsum('rd,tde->tre', low_back(norm_one), w_qkv[:, :, lo_col:hi_col], precision=HIGHEST)) for lo_col, hi_col in piece_bounds(D)], axis=2)
    queries = low(proj_all[0] + b_qv[0]).reshape(-1, HEADS, HDIM)
    keys_all = low(proj_all[1]).reshape(-1, HEADS, HDIM)
    values_all = low(proj_all[2] + b_qv[1]).reshape(-1, HEADS, HDIM)
    scores = low_back(jnp.einsum('qhe,khe->hqk', queries, keys_all, precision=HIGHEST) * HDIM ** (-0.5))
    same_seg = segment[:, None] == segment[None, :]
    scores = jnp.where(same_seg[None, :, :], scores, -1e+30)
    probs = low(jax.nn.softmax(scores, axis=-1))
    mixed_all = jnp.einsum('hqk,khe->qhe', probs, values_all, precision=HIGHEST).reshape(-1, HEADS * HDIM)
    mixed_all = low(low_back(mixed_all))
    attn_out = b_out + sum((low(low_back(jnp.einsum('re,de->rd', mixed_all[:, lo_col:hi_col], w_out[:, lo_col:hi_col], precision=HIGHEST))) for lo_col, hi_col in piece_bounds(D)))
    resid_one = tok_slot + attn_out
    norm_two = low(layer_norm(resid_one) * ln2_gain + ln2_bias)
    pre_up = jnp.concatenate([low_back(jnp.dot(low_back(norm_two), w_up[:, lo_col:hi_col], precision=HIGHEST)) for lo_col, hi_col in piece_bounds(FF)], axis=1) + b_up
    act_low = low(jax.nn.gelu(pre_up, approximate=False))
    mlp_out = b_down + sum((low(low_back(jnp.einsum('rf,df->rd', act_low[:, lo_col:hi_col], w_down[:, lo_col:hi_col], precision=HIGHEST))) for lo_col, hi_col in piece_bounds(FF)))
    block_rows = resid_one + mlp_out
    cond_low = low(jax.nn.silu(block_rows))
    mod_all = low_back(jnp.einsum('rd,tde->tre', cond_low, w_mod, precision=HIGHEST)) + b_mod[:, None, :]
    hid_in = low(layer_norm(lat_slot) * (1.0 + mod_all[1]) + mod_all[0])
    pre_hid = jnp.concatenate([low_back(jnp.dot(low_back(hid_in), w_hid1[:, lo_col:hi_col], precision=HIGHEST)) for lo_col, hi_col in piece_bounds(W)], axis=1) + b_hid1
    hidden = low(jax.nn.silu(pre_hid))
    branch = b_hid2 + sum((low(low_back(jnp.einsum('ri,oi->ro', hidden[:, lo_col:hi_col], w_hid2[:, lo_col:hi_col], precision=HIGHEST))) for lo_col, hi_col in piece_bounds(W)))
    head_branch = mod_all[2] * branch
    head_rows = lat_slot + head_branch
    row_mask = valid_row[:, None]
    stat_sums = jnp.stack([jnp.sum(row_mask * block_rows * block_rows), jnp.sum(row_mask * attn_out * attn_out), jnp.sum(row_mask * mlp_out * mlp_out), jnp.sum(row_mask * head_branch * head_branch)])
    return ((block_rows, head_rows), stat_sums)

def reference(tokens, latents, grad_block, grad_head, image_lengths, ln1_gain, ln1_bias, w_qkv, b_qv, w_out, b_out, ln2_gain, ln2_bias, w_up, b_up, w_down, b_down, w_mod, b_mod, w_hid1, b_hid1, w_hid2, b_hid2):
    params = tuple((weight.astype(jnp.float32) for weight in (ln1_gain, ln1_bias, w_qkv, b_qv, w_out, b_out, ln2_gain, ln2_bias, w_up, b_up, w_down, b_down, w_mod, b_mod, w_hid1, b_hid1, w_hid2, b_hid2)))
    slot_len = LONG + BUF
    tok_slots = tokens.astype(jnp.float32).reshape(SLOTS, slot_len, D)
    lat_slots = latents.astype(jnp.float32).reshape(SLOTS, slot_len, W)
    gblock_slots = grad_block.astype(jnp.float32).reshape(SLOTS, slot_len, D)
    ghead_slots = grad_head.astype(jnp.float32).reshape(SLOTS, slot_len, W)
    widths = jnp.array([D, D, D, W], jnp.float32)

    def one_slot(grad_sums, slot_in):
        tok_slot, lat_slot, gblock_slot, ghead_slot, lengths = slot_in
        segment, valid_row, image_row = slot_masks(lengths)

        def forward(tok_arg, lat_arg, param_arg):
            return slot_forward(tok_arg, lat_arg, param_arg, segment, valid_row)
        outputs, pullback, stat_sums = jax.vjp(forward, tok_slot, lat_slot, params, has_aux=True)
        grad_tok, grad_lat, grad_params = pullback((gblock_slot * valid_row[:, None], ghead_slot * image_row[:, None]))
        grad_sums = jax.tree.map(jnp.add, grad_sums, grad_params)
        slot_rms = jnp.sqrt(stat_sums / (jnp.sum(valid_row) * widths))
        return (grad_sums, (outputs[0], outputs[1], grad_tok, grad_lat, slot_rms))
    initial = jax.tree.map(jnp.zeros_like, params)
    grad_sums, stacked = lax.scan(one_slot, initial, (tok_slots, lat_slots, gblock_slots, ghead_slots, image_lengths))
    block_all, head_all, gtok_all, glat_all, rms_values = stacked
    return (block_all.reshape(TOKENS, D).astype(jnp.bfloat16), head_all.reshape(TOKENS, W).astype(jnp.bfloat16), gtok_all.reshape(TOKENS, D), glat_all.reshape(TOKENS, W), grad_sums[0], grad_sums[1], grad_sums[2], grad_sums[3], grad_sums[4], grad_sums[5], grad_sums[6], grad_sums[7], grad_sums[8], grad_sums[9], grad_sums[10], grad_sums[11], grad_sums[12], grad_sums[13], grad_sums[14], grad_sums[15], grad_sums[16], grad_sums[17], rms_values)
```

```python
import functools

import jax
import jax.numpy as jnp
from jax import lax
from jax.experimental import pallas as pl
from jax.experimental.pallas import tpu as pltpu
from jax.sharding import PartitionSpec as P

HDIM = 64
BUF = 64
LONG = 1024
EPS_NORM = 1e-06
FAR = -1e30
VMEM_LIMIT = 60 * 1024 * 1024
F32 = jnp.float32
LOW = jnp.bfloat16


def params():
    return pltpu.CompilerParams(vmem_limit_bytes=VMEM_LIMIT)


def dot_nn(a, b):
    return lax.dot_general(a, b, (((1,), (0,)), ((), ())), preferred_element_type=F32)


def dot_nt(a, b):
    return lax.dot_general(a, b, (((1,), (1,)), ((), ())), preferred_element_type=F32)


def dot_tn(a, b):
    return lax.dot_general(a, b, (((0,), (0,)), ((), ())), preferred_element_type=F32)


def norm_parts(values):
    row_mean = jnp.mean(values, axis=-1, keepdims=True)
    centred = values - row_mean
    inv_dev = lax.rsqrt(jnp.mean(centred * centred, axis=-1, keepdims=True) + EPS_NORM)
    return centred * inv_dev, inv_dev


def norm_back(grad_norm, normed, inv_dev):
    mean_grad = jnp.mean(grad_norm, axis=-1, keepdims=True)
    mean_cross = jnp.mean(grad_norm * normed, axis=-1, keepdims=True)
    return inv_dev * (grad_norm - mean_grad - normed * mean_cross)


def gelu_parts(x):
    z = jnp.abs(x) * 0.7071067811865476
    t = 1.0 / (1.0 + 0.3275911 * z)
    e = jnp.exp(-z * z)
    poly = t * (
        0.254829592 + t * (-0.284496736 + t * (1.421413741 + t * (-1.453152027 + t * 1.061405429)))
    )
    tail = 0.5 * poly * e
    cdf = jnp.where(x >= 0, 1.0 - tail, tail)
    return x * cdf, cdf + x * (0.3989422804014327 * e)


def sigmoid(x):
    return 0.5 * jnp.tanh(0.5 * x) + 0.5


def flat(block):
    return block.reshape(block.shape[0] * block.shape[1], block.shape[2])


def colsum(values):
    return jnp.sum(values, axis=0, keepdims=True)


def qkv_kernel(tp, tok, gain, bias, w_own, w_oth, b_own, b_oth, norm_out, proj_out):
    normed, _ = norm_parts(tok[...].astype(F32))
    norm_one = (normed * gain[...] + bias[...]).astype(LOW)
    norm_out[...] = norm_one
    half = w_own.shape[-1]
    for side, (w, b) in enumerate(((w_own, b_own), (w_oth, b_oth))):
        for t in range(3):
            proj = dot_nn(norm_one, flat(w[:, 0, t]))
            if t == 0:
                low = ((proj + b[0:1]).astype(LOW).astype(F32) * HDIM ** (-0.5)).astype(LOW)
            elif t == 1:
                low = proj.astype(LOW)
            else:
                low = (proj + b[1:2]).astype(LOW)
            proj_out[t, :, side * half : (side + 1) * half] = low


def row_spec(rows, *tail):
    zeros = (0,) * len(tail)
    return pl.BlockSpec((rows, *tail), lambda i, tp: (i, *zeros))


def const_spec(*shape):
    zeros = (0,) * len(shape)
    return pl.BlockSpec(shape, lambda i, tp: zeros, pipeline_mode=pl.Buffered(1))


def side_spec(arr, count, first, other):
    dp, _, _, rows, cols = arr.shape
    block = (dp, 1, count, rows, cols)
    if other:
        return pl.BlockSpec(
            block, lambda i, tp: (0, 1 - tp[0], first // count, 0, 0), pipeline_mode=pl.Buffered(1)
        )
    return pl.BlockSpec(
        block, lambda i, tp: (0, tp[0], first // count, 0, 0), pipeline_mode=pl.Buffered(1)
    )


def sds(shape, dtype):
    return jax.ShapeDtypeStruct(shape, dtype)


def run(kernel, tp, steps, ins, outs, scratch=(), flops=0, nbytes=0, exps=0):
    return pl.pallas_call(
        kernel,
        grid_spec=pltpu.PrefetchScalarGridSpec(
            num_scalar_prefetch=1,
            grid=(steps,),
            in_specs=[spec for _, spec in ins],
            out_specs=[spec for _, spec in outs],
            scratch_shapes=list(scratch),
        ),
        out_shape=[shape for shape, _ in outs],
        compiler_params=params(),
        cost_estimate=pl.CostEstimate(flops=flops, bytes_accessed=nbytes, transcendentals=exps),
    )(tp, *[arr for arr, _ in ins])


def lanes():
    return lax.broadcasted_iota(jnp.int32, (1, 128), 1)


def attn_fwd_kernel(tp, q, k, v, seg_q, seg_k, mixed, total):
    rows = q.shape[0]
    chunk = rows // 4
    left = lanes() < HDIM
    k_all, v_all = k[...], v[...]
    one = jnp.ones_like(v_all)
    k_aug = (jnp.where(left, k_all, seg_k[...]), jnp.where(left, seg_k[...], k_all))
    v_aug = (jnp.where(left, v_all, one), jnp.where(left, one, v_all))

    def step(i, carry):
        at = pl.ds(pl.multiple_of(i * chunk, 16), chunk)
        q_part, seg_part = q[at, :], seg_q[at, :]
        q_aug = (jnp.where(left, q_part, seg_part), jnp.where(left, seg_part, q_part))
        outs = []
        for h in range(2):
            s = dot_nt(q_aug[h], k_aug[h])
            top = jnp.max(s, axis=1, keepdims=True)
            p = jnp.exp(s - top).astype(LOW)
            outs.append((dot_nn(p, v_aug[h]), top))
        mix = jnp.where(left, outs[0][0], outs[1][0])
        tot = jnp.where(left, outs[1][0], outs[0][0])
        tot = pltpu.roll(tot, HDIM, 1)
        mixed[at, :] = (mix / tot).astype(LOW)
        total[at, :] = jnp.where(left, outs[0][1], outs[1][1]) + jnp.log(tot)
        return carry

    lax.fori_loop(0, 4, step, 0)


def three_terms(value, at, base):
    lane = lanes() & (HDIM - 1)
    hi = value.astype(LOW)
    rest = value - hi.astype(F32)
    mid = rest.astype(LOW)
    low = (rest - mid.astype(F32)).astype(LOW)
    out = jnp.where(lane == at, hi, base)
    out = jnp.where(lane == at + 1, mid, out)
    return jnp.where(lane == at + 2, low, out)


def attn_bwd_kernel(
    tp, q, k, v, g, mixed, total, seg_q, seg_k, dproj, sums, q0, q1, g0, g1, dq_t
):
    rows = q.shape[0]
    chunk = rows // 4
    left = lanes() < HDIM
    lane = lanes() & (HDIM - 1)
    q_all, g_all = q[...], g[...]
    cross = g_all.astype(F32) * mixed[...].astype(F32)
    d_left = jnp.sum(jnp.where(left, cross, 0.0), axis=1, keepdims=True)
    d_right = jnp.sum(jnp.where(left, 0.0, cross), axis=1, keepdims=True)
    neg_total = -pltpu.roll(total[...], HDIM, 1)
    q_tail = three_terms(neg_total, 4, seg_q[...])
    g_tail = three_terms(
        jnp.where(left, -d_right, -d_left), 0, jnp.zeros_like(g_all)
    )
    q0[...] = jnp.where(left, q_all, q_tail)
    q1[...] = jnp.where(left, q_tail, q_all)
    g0[...] = jnp.where(left, g_all, g_tail)
    g1[...] = jnp.where(left, g_tail, g_all)
    dq_t[...] = jnp.zeros_like(dq_t)
    k_ones = jnp.where((lane >= 4) & (lane < 7), 1.0, 0.0).astype(LOW)
    v_ones = jnp.where(lane < 3, 1.0, 0.0).astype(LOW)
    sums[...] = jnp.zeros_like(sums)

    def step(i, carry):
        at = pl.ds(pl.multiple_of(i * chunk, 16), chunk)
        k_part, v_part = k[at, :], v[at, :]
        k_tail = seg_k[at, :] + k_ones
        v_tail = jnp.broadcast_to(v_ones, v_part.shape)
        zero = jnp.zeros_like(k_part)
        dk, dv = [], []
        for h, (q_aug, g_aug) in enumerate(((q0, g0), (q1, g1))):
            mine = left if h == 0 else jnp.logical_not(left)
            k_aug = jnp.where(mine, k_part, k_tail)
            v_aug = jnp.where(mine, v_part, v_tail)
            p = jnp.exp(dot_nt(k_aug, q_aug[...]))
            ds = (p * dot_nt(v_aug, g_aug[...])).astype(LOW)
            dv.append(dot_nn(p.astype(LOW), g[...]))
            dk.append(dot_nn(ds, q[...]))
            k_mine = jnp.where(mine, k_part, zero).astype(F32).T.astype(LOW)
            dq_t[...] += dot_nn(k_mine, ds)
        dk = jnp.where(left, dk[0], dk[1])
        dv = jnp.where(left, dv[0], dv[1])
        dproj[1, at, :] = dk.astype(LOW)
        dproj[2, at, :] = dv.astype(LOW)
        sums[1:2, :] += colsum(dv)
        return carry

    lax.fori_loop(0, 4, step, 0)
    dq = dq_t[...].T * HDIM ** (-0.5)
    dproj[0] = dq.astype(LOW)
    sums[0:1, :] = colsum(dq)


def ff_fwd_kernel(
    tp, tok, mixed, valid, wo_own, wo_oth, wu_own, wu_oth, wd_own, wd_oth,
    b_out, gain, bias, b_up, b_down,
    norm_two_out, normed_out, inv_out, act_out, slope_out, block_out, low_out, stats, acc,
):
    half = wo_own.shape[-1]
    ff = wu_own.shape[-1]
    wide = 512
    attn = (
        dot_nt(mixed[:, :half], flat(wo_own[:, 0, 0]))
        + dot_nt(mixed[:, half:], flat(wo_oth[:, 0, 0]))
        + b_out[...]
    )
    resid = tok[...].astype(F32) + attn
    normed, inv = norm_parts(resid)
    norm_two_out[...] = (normed * gain[...] + bias[...]).astype(LOW)
    normed_out[...] = normed.astype(LOW)
    inv_out[...] = inv
    acc[...] = jnp.zeros_like(acc)
    for side, (wu, wd) in enumerate(((wu_own, wd_own), (wu_oth, wd_oth))):

        def step(c, carry):
            at = pl.ds(pl.multiple_of(c * wide, wide), wide)
            to = pl.ds(pl.multiple_of(side * ff + c * wide, wide), wide)
            pre = dot_nn(norm_two_out[...], flat(wu[:, 0, 0, :, at])) + b_up[side : side + 1, at]
            act, slope = gelu_parts(pre)
            act = act.astype(LOW)
            if side == 0:
                act_out[:, at] = act
            slope_out[:, to] = slope.astype(LOW)
            acc[...] += dot_nt(act, flat(wd[:, 0, 0, :, at]))
            return carry

        lax.fori_loop(0, ff // wide, step, 0)
    mlp = acc[...] + b_down[...]
    block = resid + mlp
    block_out[...] = block
    low_out[...] = block.astype(LOW)

    @pl.when(pl.program_id(0) == 0)
    def _():
        stats[...] = jnp.zeros_like(stats)

    mask = valid[:, 0:1]
    stats[0:1, :] += colsum(block * block * mask)
    stats[1:2, :] += colsum(attn * attn * mask)
    stats[2:3, :] += colsum(mlp * mlp * mask)


def head_kernel(
    tp, block, lat, g_block, g_head, masks, w_mod, h1_own, h1_oth, h2_own, h2_oth,
    b_mod, b_hid1, b_hid2,
    head_out, g_lat, hid_in_out, hidden_out, branch_low_out, pre_low_out, mod_low_out, cond_out,
    dblock_out, dblock_low_out, sums_w, sums_h, sums_d,
):
    half = h1_own.shape[-1]
    valid, image = masks[:, 0:1], masks[:, 1:2]
    blk = block[...]
    sig_b = sigmoid(blk)
    cond = (blk * sig_b).astype(LOW)
    cond_out[...] = cond
    lat_in = lat[...].astype(F32)
    lat_norm, lat_inv = norm_parts(lat_in)
    shift = dot_nn(cond, flat(w_mod[:, 0])) + b_mod[0:1]
    scale = 1.0 + (dot_nn(cond, flat(w_mod[:, 1])) + b_mod[1:2])
    gate = dot_nn(cond, flat(w_mod[:, 2])) + b_mod[2:3]
    hid_in = (lat_norm * scale + shift).astype(LOW)
    hid_in_out[...] = hid_in
    branch = b_hid2[...]
    slopes = []
    for side, (h1, h2) in enumerate(((h1_own, h2_own), (h1_oth, h2_oth))):
        pre = dot_nn(hid_in, flat(h1[:, 0, 0])) + b_hid1[side : side + 1]
        sig = sigmoid(pre)
        hidden = (pre * sig).astype(LOW)
        slopes.append(sig * (1.0 + pre * (1.0 - sig)))
        if side == 0:
            hidden_out[...] = hidden
        branch = branch + dot_nt(hidden, flat(h2[:, 0, 0]))
    head_branch = gate * branch
    head_out[...] = (lat_in + head_branch).astype(LOW)
    gh = g_head[...].astype(F32) * image
    dbranch = gh * gate
    branch_low = dbranch.astype(LOW)
    branch_low_out[...] = branch_low
    dgate = gh * branch

    @pl.when(pl.program_id(0) == 0)
    def _():
        sums_w[...] = jnp.zeros_like(sums_w)
        sums_h[...] = jnp.zeros_like(sums_h)
        sums_d[...] = jnp.zeros_like(sums_d)

    dhid_in = None
    for side, (h1, h2) in enumerate(((h1_own, h2_own), (h1_oth, h2_oth))):
        dpre = dot_nn(branch_low, flat(h2[:, 0, 0])) * slopes[side]
        pre_low = dpre.astype(LOW)
        if side == 0:
            pre_low_out[...] = pre_low
            sums_h[0:1, :] += colsum(dpre)
        part = dot_nt(pre_low, flat(h1[:, 0, 0]))
        dhid_in = part if dhid_in is None else dhid_in + part
    dscale = dhid_in * lat_norm
    low0, low1, low2 = dhid_in.astype(LOW), dscale.astype(LOW), dgate.astype(LOW)
    mod_low_out[0] = low0
    mod_low_out[1] = low1
    mod_low_out[2] = low2
    sums_w[0:1, :] += colsum(dbranch)
    sums_w[1:2, :] += colsum(dhid_in)
    sums_w[2:3, :] += colsum(dscale)
    sums_w[3:4, :] += colsum(dgate)
    sums_w[4:5, :] += colsum(head_branch * head_branch * valid)
    dcond = (
        dot_nt(low0, flat(w_mod[:, 0]))
        + dot_nt(low1, flat(w_mod[:, 1]))
        + dot_nt(low2, flat(w_mod[:, 2]))
    )
    g_lat[...] = gh + norm_back(dhid_in * scale, lat_norm, lat_inv)
    dblock = g_block[...].astype(F32) * valid + dcond * (sig_b * (1.0 + blk * (1.0 - sig_b)))
    dblock_out[...] = dblock
    dblock_low_out[...] = dblock.astype(LOW)
    sums_d[0:1, :] += colsum(dblock)


def ff_bwd_kernel(
    tp, dblock, dblock_low, slope, normed_in, inv_in, wo_own, wo_oth, wu_own, wu_oth, wd_own,
    wd_oth, gain,
    dup_out, dresid_out, dresid_low_out, dmixed_out, sums_u, sums_d, acc,
):
    half = wo_own.shape[-1]
    ff = wu_own.shape[-1]
    wide = 512

    @pl.when(pl.program_id(0) == 0)
    def _():
        sums_u[...] = jnp.zeros_like(sums_u)
        sums_d[...] = jnp.zeros_like(sums_d)

    acc[...] = jnp.zeros_like(acc)
    for side, (wu, wd) in enumerate(((wu_own, wd_own), (wu_oth, wd_oth))):

        def step(c, carry):
            at = pl.ds(pl.multiple_of(c * wide, wide), wide)
            frm = pl.ds(pl.multiple_of(side * ff + c * wide, wide), wide)
            dact = dot_nn(dblock_low[...], flat(wd[:, 0, 0, :, at]))
            dpre = dact * slope[:, frm].astype(F32)
            dup = dpre.astype(LOW)
            if side == 0:
                dup_out[:, at] = dup
                sums_u[0:1, at] += colsum(dpre)
            acc[...] += dot_nt(dup, flat(wu[:, 0, 0, :, at]))
            return carry

        lax.fori_loop(0, ff // wide, step, 0)
    dnorm = acc[...]
    normed = normed_in[...].astype(F32)
    sums_d[0:1, :] += colsum(dnorm * normed)
    sums_d[1:2, :] += colsum(dnorm)
    dresid = dblock[...] + norm_back(dnorm * gain[...], normed, inv_in[...])
    sums_d[2:3, :] += colsum(dresid)
    dresid_out[...] = dresid
    low = dresid.astype(LOW)
    dresid_low_out[...] = low
    dmixed_out[:, :half] = dot_nn(low, flat(wo_own[:, 0, 0])).astype(LOW)
    dmixed_out[:, half:] = dot_nn(low, flat(wo_oth[:, 0, 0])).astype(LOW)


def tok_bwd_kernel(tp, tok, dproj, dresid, w_own, w_oth, gain, g_tok, sums):
    half = w_own.shape[-1]
    dnorm = None
    for side, w in enumerate((w_own, w_oth)):
        for t in range(3):
            part = dot_nt(dproj[t, :, side * half : (side + 1) * half], flat(w[:, 0, t]))
            dnorm = part if dnorm is None else dnorm + part
    normed, inv = norm_parts(tok[...].astype(F32))

    @pl.when(pl.program_id(0) == 0)
    def _():
        sums[...] = jnp.zeros_like(sums)

    sums[0:1, :] += colsum(dnorm * normed)
    sums[1:2, :] += colsum(dnorm)
    g_tok[...] = dresid[...] + norm_back(dnorm * gain[...], normed, inv)


def slot_masks(lengths):
    bounds = jnp.cumsum(lengths)
    positions = jnp.arange(LONG + BUF, dtype=jnp.int32)
    segment = jnp.sum((positions[:, None] >= bounds[None, :]).astype(jnp.int32), axis=1)
    starts = jnp.concatenate([jnp.zeros((1,), jnp.int32), bounds])
    first_row = jnp.sum(
        jnp.where(segment[:, None] == jnp.arange(4, dtype=jnp.int32)[None, :], starts[None, :], 0),
        axis=1,
    )
    valid_row = positions < bounds[2]
    image_row = valid_row & (positions - first_row >= BUF)
    return (segment, valid_row.astype(F32), image_row.astype(F32))


def gather(group):
    full = lax.all_gather(group, ("dp", "tp"), axis=0)
    return full.reshape(-1, 2, *group.shape)


def both_sides(mine):
    other = lax.ppermute(mine, "tp", [(0, 1), (1, 0)])
    return jnp.stack([mine, other])


def on_device(
    tokens, latents, grad_block, grad_head, image_lengths, ln1_gain, ln1_bias, w_qkv, b_qv, w_out,
    b_out, ln2_gain, ln2_bias, w_up, b_up, w_down, b_down, w_mod, b_mod, w_hid1, b_hid1, w_hid2,
    b_hid2,
):
    rows, width = tokens.shape
    head_width = latents.shape[1]
    half = w_qkv.shape[2]
    ff = w_up.shape[1]
    hid = w_hid1.shape[1]
    n_dp = width // w_out.shape[0]
    tp = lax.axis_index("tp").reshape(1)
    pairs = 2 * half // 128
    tall = rows // 2
    steps = rows // tall
    short = rows // 4
    vec = lambda v: v.reshape(1, -1)

    g_attn = gather(jnp.concatenate([w_qkv, w_out[None]]))
    g_ff = gather(jnp.stack([w_up, w_down]))
    g_mod = lax.all_gather(w_mod, "dp", axis=0)
    g_hid = gather(jnp.stack([w_hid1, w_hid2]))
    small = both_sides(jnp.concatenate([b_qv.reshape(-1), b_up, b_hid1]))
    b_qv2 = small[:, : 2 * half].reshape(2, 2, half)
    b_up2 = small[:, 2 * half : 2 * half + ff]
    b_hid2x = small[:, 2 * half + ff :]

    segment, valid_row, image_row = slot_masks(image_lengths[0])
    masks = jnp.stack([valid_row, image_row], axis=1)
    lane_of = (jnp.arange(128) % HDIM)[None, :]
    same = segment[:, None] == lane_of
    seg_q = jnp.where(same & (lane_of < 4), 1.0, 0.0).astype(LOW)
    seg_k = jnp.where(jnp.logical_not(same) & (lane_of < 4), FAR, 0.0).astype(LOW)

    norm_one, proj = run(
        qkv_kernel, tp, steps,
        [
            (tokens, row_spec(tall, width)),
            (vec(ln1_gain), const_spec(1, width)),
            (vec(ln1_bias), const_spec(1, width)),
            (g_attn, pl.BlockSpec((n_dp, 1, 3, *g_attn.shape[3:]), lambda i, tp: (0, tp[0], 0, 0, 0), pipeline_mode=pl.Buffered(1))),
            (g_attn, pl.BlockSpec((n_dp, 1, 3, *g_attn.shape[3:]), lambda i, tp: (0, 1 - tp[0], 0, 0, 0), pipeline_mode=pl.Buffered(1))),
            (b_qv2[0], const_spec(2, half)),
            (b_qv2[1], const_spec(2, half)),
        ],
        [
            (sds((rows, width), LOW), row_spec(tall, width)),
            (sds((3, rows, width), LOW), pl.BlockSpec((3, tall, width), lambda i, tp: (0, i, 0))),
        ],
        flops=2 * rows * width * 3 * width,
        nbytes=10 * rows * width,
    )

    def part_spec(t):
        return pl.BlockSpec((None, rows, 128), lambda p, tp: (t, 0, p))

    pair_spec = pl.BlockSpec((rows, 128), lambda p, tp: (0, p))
    whole = pl.BlockSpec((rows, 128), lambda p, tp: (0, 0))
    mixed, total = run(
        attn_fwd_kernel, tp, pairs,
        [
            (proj, part_spec(0)), (proj, part_spec(1)), (proj, part_spec(2)),
            (seg_q, whole), (seg_k, whole),
        ],
        [
            (sds((rows, width), LOW), pair_spec),
            (sds((rows, width), F32), pair_spec),
        ],
        flops=4 * rows * rows * 256 * 2 * pairs,
        nbytes=12 * rows * width,
        exps=2 * pairs * rows * rows,
    )

    ff_weights = [
        (g_attn, side_spec(g_attn, 1, 3, False)), (g_attn, side_spec(g_attn, 1, 3, True)),
        (g_ff, side_spec(g_ff, 1, 0, False)), (g_ff, side_spec(g_ff, 1, 0, True)),
        (g_ff, side_spec(g_ff, 1, 1, False)), (g_ff, side_spec(g_ff, 1, 1, True)),
    ]
    norm_two, normed_two, inv_two, act, slope, block, block_low, stats = run(
        ff_fwd_kernel, tp, rows // tall,
        [
            (tokens, row_spec(tall, width)), (mixed, row_spec(tall, width)),
            (masks, row_spec(tall, 2)), *ff_weights,
            (vec(b_out), const_spec(1, width)), (vec(ln2_gain), const_spec(1, width)),
            (vec(ln2_bias), const_spec(1, width)), (b_up2, const_spec(2, ff)),
            (vec(b_down), const_spec(1, width)),
        ],
        [
            (sds((rows, width), LOW), row_spec(tall, width)),
            (sds((rows, width), LOW), row_spec(tall, width)),
            (sds((rows, 1), F32), row_spec(tall, 1)),
            (sds((rows, ff), LOW), row_spec(tall, ff)),
            (sds((rows, 2 * ff), LOW), row_spec(tall, 2 * ff)),
            (sds((rows, width), F32), row_spec(tall, width)),
            (sds((rows, width), LOW), row_spec(tall, width)),
            (sds((8, width), F32), pl.BlockSpec((8, width), lambda i, tp: (0, 0))),
        ],
        scratch=[pltpu.VMEM((tall, width), F32)],
        flops=2 * rows * width * (4 * ff + width),
        nbytes=rows * (20 * width + 6 * ff) + 8 * width * ff,
        exps=4 * rows * ff,
    )

    keep = lambda n, w: (sds((n, w), F32), pl.BlockSpec((n, w), lambda i, tp: (0, 0)))
    (
        head_out, grad_latents, hid_in, hidden, branch_low, pre_low, mod_low, cond, dblock,
        dblock_low, sums_w, sums_h, sums_b,
    ) = run(
        head_kernel, tp, rows // short,
        [
            (block, row_spec(short, width)), (latents, row_spec(short, head_width)),
            (grad_block, row_spec(short, width)), (grad_head, row_spec(short, head_width)),
            (masks, row_spec(short, 2)), (g_mod, const_spec(*g_mod.shape)),
            (g_hid, side_spec(g_hid, 1, 0, False)), (g_hid, side_spec(g_hid, 1, 0, True)),
            (g_hid, side_spec(g_hid, 1, 1, False)), (g_hid, side_spec(g_hid, 1, 1, True)),
            (b_mod, const_spec(3, head_width)), (b_hid2x, const_spec(2, hid)),
            (vec(b_hid2), const_spec(1, head_width)),
        ],
        [
            (sds((rows, head_width), LOW), row_spec(short, head_width)),
            (sds((rows, head_width), F32), row_spec(short, head_width)),
            (sds((rows, head_width), LOW), row_spec(short, head_width)),
            (sds((rows, hid), LOW), row_spec(short, hid)),
            (sds((rows, head_width), LOW), row_spec(short, head_width)),
            (sds((rows, hid), LOW), row_spec(short, hid)),
            (sds((3, rows, head_width), LOW), pl.BlockSpec((3, short, head_width), lambda i, tp: (0, i, 0))),
            (sds((rows, width), LOW), row_spec(short, width)),
            (sds((rows, width), F32), row_spec(short, width)),
            (sds((rows, width), LOW), row_spec(short, width)),
            keep(8, head_width), keep(8, hid), keep(8, width),
        ],
        flops=2 * rows * head_width * (6 * width + 4 * head_width),
        nbytes=rows * (14 * width + 22 * head_width) + 20 * head_width * head_width,
        exps=rows * 2 * head_width,
    )

    dup, dresid, dresid_low, dmixed, sums_u, sums_r = run(
        ff_bwd_kernel, tp, rows // tall,
        [
            (dblock, row_spec(tall, width)), (dblock_low, row_spec(tall, width)),
            (slope, row_spec(tall, 2 * ff)), (normed_two, row_spec(tall, width)),
            (inv_two, row_spec(tall, 1)), *ff_weights, (vec(ln2_gain), const_spec(1, width)),
        ],
        [
            (sds((rows, ff), LOW), row_spec(tall, ff)),
            (sds((rows, width), F32), row_spec(tall, width)),
            (sds((rows, width), LOW), row_spec(tall, width)),
            (sds((rows, width), LOW), row_spec(tall, width)),
            keep(8, ff), keep(8, width),
        ],
        scratch=[pltpu.VMEM((tall, width), F32)],
        flops=2 * rows * width * (4 * ff + width),
        nbytes=rows * (16 * width + 6 * ff) + 8 * width * ff,
    )

    dproj, sums_qv = run(
        attn_bwd_kernel, tp, pairs,
        [
            (proj, part_spec(0)), (proj, part_spec(1)), (proj, part_spec(2)),
            (dmixed, pair_spec), (mixed, pair_spec), (total, pair_spec),
            (seg_q, whole), (seg_k, whole),
        ],
        [
            (sds((3, rows, width), LOW), pl.BlockSpec((3, rows, 128), lambda p, tp: (0, 0, p))),
            (sds((8, width), F32), pl.BlockSpec((8, 128), lambda p, tp: (0, p))),
        ],
        scratch=[pltpu.VMEM((rows, 128), LOW)] * 4 + [pltpu.VMEM((128, rows), F32)],
        flops=10 * rows * rows * 256 * 2 * pairs,
        nbytes=20 * rows * width,
        exps=2 * pairs * rows * rows,
    )
    grad_tokens, sums_t = run(
        tok_bwd_kernel, tp, steps,
        [
            (tokens, row_spec(tall, width)),
            (dproj, pl.BlockSpec((3, tall, width), lambda i, tp: (0, i, 0))),
            (dresid, row_spec(tall, width)),
            (g_attn, pl.BlockSpec((n_dp, 1, 3, *g_attn.shape[3:]), lambda i, tp: (0, tp[0], 0, 0, 0), pipeline_mode=pl.Buffered(1))),
            (g_attn, pl.BlockSpec((n_dp, 1, 3, *g_attn.shape[3:]), lambda i, tp: (0, 1 - tp[0], 0, 0, 0), pipeline_mode=pl.Buffered(1))),
            (vec(ln1_gain), const_spec(1, width)),
        ],
        [(sds((rows, width), F32), row_spec(tall, width)), keep(8, width)],
        flops=2 * rows * width * 3 * width,
        nbytes=16 * rows * width,
    )

    def scatter(parts):
        packed = [p.astype(LOW).reshape(n_dp, -1, p.shape[-1]) for p in parts]
        packed = jnp.concatenate(packed, axis=1)
        return lax.psum_scatter(packed, "dp", scatter_dimension=0, tiled=False).astype(F32)

    def by_shard(stacked):
        n, depth, cols = stacked.shape
        return jnp.transpose(stacked.reshape(n, n_dp, depth // n_dp, cols), (1, 0, 2, 3)).reshape(
            -1, cols
        )

    mod_half = head_width // 2
    mod_own = lax.dynamic_slice_in_dim(mod_low, tp[0] * mod_half, mod_half, axis=2)
    d_hid2 = dot_tn(branch_low, hidden)
    d_hid1 = dot_tn(hid_in, pre_low)
    d_mod = jnp.einsum("rd,tre->tde", cond, mod_own, preferred_element_type=F32)
    got = scatter([d_hid1, d_hid2, by_shard(d_mod.astype(LOW))])
    in_rows = head_width // n_dp
    d_w_hid1, d_w_hid2 = got[:in_rows], got[in_rows : 2 * in_rows]
    mine = got[2 * in_rows :].reshape(3, -1, mod_half)
    theirs = lax.ppermute(mine, "tp", [(0, 1), (1, 0)])
    first = tp[0] == 0
    d_w_mod = jnp.concatenate(
        [jnp.where(first, mine, theirs), jnp.where(first, theirs, mine)], axis=2
    )
    d_down = dot_tn(dblock_low, act)
    d_up = dot_tn(norm_two, dup)
    got = scatter([d_down, d_up])
    w_rows = width // n_dp
    d_w_down, d_w_up = got[:w_rows], got[w_rows:]
    d_out = dot_tn(dresid_low, mixed[:, :half])
    d_qkv = jnp.einsum("rd,tre->tde", norm_one, dproj[:, :, :half], preferred_element_type=F32)
    got = scatter([d_out, by_shard(d_qkv.astype(LOW))])
    d_w_out = got[:w_rows]
    d_w_qkv = got[w_rows:].reshape(3, w_rows, half)

    pieces = [
        sums_t[0:2].reshape(-1), sums_qv[0:2, :half].reshape(-1), sums_r[0:3].reshape(-1),
        sums_u[0], sums_b[0], sums_w[0:4].reshape(-1), sums_h[0],
    ]
    sizes = [p.shape[0] for p in pieces]
    joined = jnp.concatenate(pieces)
    joined = jnp.pad(joined, (0, -joined.shape[0] % 1024)).reshape(-1, 128)
    summed = jnp.sum(lax.all_gather(joined, "dp", axis=0), axis=0).reshape(-1)
    ends, at = [], 0
    for size in sizes:
        ends.append(summed[at : at + size])
        at += size
    ln1s, bqv, rs, d_b_up, d_b_down, ws, d_b_hid1 = ends
    ln1s, bqv, rs = ln1s.reshape(2, -1), bqv.reshape(2, -1), rs.reshape(3, -1)
    ws = ws.reshape(4, -1)

    squares = jnp.concatenate([jnp.sum(stats[0:3], axis=1), jnp.sum(sums_w[4:5], axis=1)])
    widths = jnp.array([width, width, width, head_width], F32)
    rms_values = jnp.sqrt(squares / (jnp.sum(valid_row) * widths)).reshape(1, 4)
    return (
        block_low, head_out, grad_tokens, grad_latents, ln1s[0], ln1s[1], d_w_qkv, bqv, d_w_out,
        rs[2], rs[0], rs[1], d_w_up, d_b_up, d_w_down, d_b_down, d_w_mod, ws[1:4], d_w_hid1,
        d_b_hid1, d_w_hid2, ws[0], rms_values,
    )


def solution(mesh):
    rows, one = P("dp", None), P()
    split = P("dp", "tp")
    weights = (
        one, one, P(None, "dp", "tp"), P(None, "tp"), split, one, one, one, split, P("tp"), split,
        one, P(None, "dp", None), one, split, P("tp"), split, one,
    )
    return jax.shard_map(
        on_device,
        mesh=mesh,
        in_specs=(rows, rows, rows, rows, rows) + weights,
        out_specs=(rows, rows, rows, rows) + weights + (rows,),
        check_vma=False,
    )
```

```python
import jax
import jax.numpy as jnp
from jax import lax
from jax.experimental import pallas as pl
from jax.experimental.pallas import tpu as pltpu
from jax.sharding import PartitionSpec as P

HDIM = 64
BUF = 64
LONG = 1024
EPS_NORM = 1e-06
FAR = -1e30
VMEM_LIMIT = 60 * 1024 * 1024
F32 = jnp.float32
LOW = jnp.bfloat16


def params():
    return pltpu.CompilerParams(vmem_limit_bytes=VMEM_LIMIT)


def dot_nn(a, b):
    return lax.dot_general(a, b, (((1,), (0,)), ((), ())), preferred_element_type=F32)


def dot_nt(a, b):
    return lax.dot_general(a, b, (((1,), (1,)), ((), ())), preferred_element_type=F32)


def dot_tn(a, b):
    return lax.dot_general(a, b, (((0,), (0,)), ((), ())), preferred_element_type=F32)


def norm_parts(values):
    row_mean = jnp.mean(values, axis=-1, keepdims=True)
    centred = values - row_mean
    inv_dev = lax.rsqrt(jnp.mean(centred * centred, axis=-1, keepdims=True) + EPS_NORM)
    return centred * inv_dev, inv_dev


def norm_back(grad_norm, normed, inv_dev):
    mean_grad = jnp.mean(grad_norm, axis=-1, keepdims=True)
    mean_cross = jnp.mean(grad_norm * normed, axis=-1, keepdims=True)
    return inv_dev * (grad_norm - mean_grad - normed * mean_cross)


TANH_POLY = (
    1.75632313e-09, -1.32267789e-07, 3.96479041e-06, -5.53064013e-05, -3.25945666e-05,
    3.63330843e-02, 7.97884942e-01,
)


def gelu_parts(x):
    u = x * x
    poly = TANH_POLY[0]
    for term in TANH_POLY[1:]:
        poly = poly * u + term
    cdf = 0.5 * jnp.tanh(x * poly) + 0.5
    bell = jnp.exp2(u * -0.7213475204444817)
    return x * cdf, cdf + (x * 0.3989422804014327) * bell


def sigmoid(x):
    return 0.5 * jnp.tanh(0.5 * x) + 0.5


def flat(block):
    rows = 1
    for size in block.shape[:-1]:
        rows *= size
    return block.reshape(rows, block.shape[-1])


def colsum(values):
    return jnp.sum(values, axis=0, keepdims=True)


SHARDS = 16
TP, CORE, ENDS = 0, 1, 2


def row_spec(rows, *tail):
    zeros = (0,) * len(tail)
    return pl.BlockSpec((rows, *tail), lambda i, meta: (i, *zeros))


def const_spec(*shape):
    zeros = (0,) * len(shape)
    return pl.BlockSpec(shape, lambda i, meta: zeros, pipeline_mode=pl.Buffered(1))


def sum_spec(rows, cols):
    return pl.BlockSpec((rows, cols), lambda i, meta: (0, 0))


ANY = pl.BlockSpec(memory_space=pl.ANY)


def sds(shape, dtype):
    return jax.ShapeDtypeStruct(shape, dtype)


def run(kernel, meta, steps, ins, outs, scratch=(), flops=0, nbytes=0, exps=0):
    return pl.pallas_call(
        kernel,
        grid_spec=pltpu.PrefetchScalarGridSpec(
            num_scalar_prefetch=1,
            grid=(steps,),
            in_specs=[spec for _, spec in ins],
            out_specs=[spec for _, spec in outs],
            scratch_shapes=list(scratch),
        ),
        out_shape=[shape for shape, _ in outs],
        compiler_params=params(),
        cost_estimate=pl.CostEstimate(flops=flops, bytes_accessed=nbytes, transcendentals=exps),
    )(meta, *[arr for arr, _ in ins])


def fetch(meta, pair, at, count, into, sems):
    core = meta[CORE]
    return [
        pltpu.make_async_copy(ref.at[:, at : at + count, :], into.at[:, side], sems.at[i])
        for i, (ref, side) in enumerate(zip(pair, (core, 1 - core)))
    ]


def in_first_step(copies, act):
    @pl.when(pl.program_id(0) == 0)
    def _():
        for copy in copies:
            getattr(copy, act)()


def row_masks(meta, rows):
    at = pl.program_id(0) * rows + lax.broadcasted_iota(jnp.int32, (rows, 1), 0)
    e0, e1, e2 = meta[ENDS], meta[ENDS + 1], meta[ENDS + 2]
    first = jnp.where(at < e0, 0, jnp.where(at < e1, e0, jnp.where(at < e2, e1, e2)))
    valid = at < e2
    image = valid & (at - first >= BUF)
    return jnp.where(valid, 1.0, 0.0), jnp.where(image, 1.0, 0.0)


def project(norm_one, w, bias, proj_out):
    half = w.shape[-1]
    rows = w.shape[2] // 3
    for t in range(3):
        proj = dot_nn(norm_one, flat(w[:, :, t * rows : (t + 1) * rows, :]))
        if t == 0:
            low = ((proj + bias[0:1, :half]).astype(LOW).astype(F32) * HDIM ** (-0.5)).astype(LOW)
        elif t == 1:
            low = proj.astype(LOW)
        else:
            low = (proj + bias[1:2, :half]).astype(LOW)
        proj_out[t] = low


def qkv_own_kernel(meta, tok, vecs, w0, w1, b_qv, norm_out, proj_out, w, sems):
    copies = fetch(meta, (w0, w1), 0, w.shape[2], w, sems)
    in_first_step(copies, "start")
    normed, _ = norm_parts(tok[...].astype(F32))
    norm_one = (normed * vecs[0:1] + vecs[1:2]).astype(LOW)
    norm_out[...] = norm_one
    in_first_step(copies, "wait")
    project(norm_one, w, b_qv, proj_out)


def qkv_other_kernel(meta, norm_one, w0, w1, b_qv, proj_out, w, sems):
    copies = fetch(meta, (w0, w1), 0, w.shape[2], w, sems)
    in_first_step(copies, "start")
    in_first_step(copies, "wait")
    project(norm_one[...], w, b_qv, proj_out)


def lanes():
    return lax.broadcasted_iota(jnp.int32, (1, 128), 1)


def attn_fwd_kernel(meta, q, k, v, seg_q, seg_k, mixed, total):
    rows = q.shape[0]
    chunk = rows // 4
    left = lanes() < HDIM
    k_all, v_all = k[...], v[...]
    one = jnp.ones_like(v_all)
    k_aug = (jnp.where(left, k_all, seg_k[...]), jnp.where(left, seg_k[...], k_all))
    v_aug = (jnp.where(left, v_all, one), jnp.where(left, one, v_all))

    def step(i, carry):
        at = pl.ds(pl.multiple_of(i * chunk, 16), chunk)
        q_part, seg_part = q[at, :], seg_q[at, :]
        q_aug = (jnp.where(left, q_part, seg_part), jnp.where(left, seg_part, q_part))
        outs = []
        for h in range(2):
            s = dot_nt(q_aug[h], k_aug[h])
            top = jnp.max(s, axis=1, keepdims=True)
            p = jnp.exp(s - top).astype(LOW)
            outs.append((dot_nn(p, v_aug[h]), top))
        mix = jnp.where(left, outs[0][0], outs[1][0])
        tot = jnp.where(left, outs[1][0], outs[0][0])
        tot = pltpu.roll(tot, HDIM, 1)
        mixed[at, :] = (mix / tot).astype(LOW)
        total[at, :] = jnp.where(left, outs[0][1], outs[1][1]) + jnp.log(tot)
        return carry

    lax.fori_loop(0, 4, step, 0, unroll=True)


def three_terms(value, at, base):
    lane = lanes() & (HDIM - 1)
    hi = value.astype(LOW)
    rest = value - hi.astype(F32)
    mid = rest.astype(LOW)
    low = (rest - mid.astype(F32)).astype(LOW)
    out = jnp.where(lane == at, hi, base)
    out = jnp.where(lane == at + 1, mid, out)
    return jnp.where(lane == at + 2, low, out)


def attn_bwd_kernel(meta, q, k, v, g, mixed, total, seg_q, seg_k, dproj, sums):
    left = lanes() < HDIM
    lane = lanes() & (HDIM - 1)
    q_all, k_all, v_all, g_all = q[...], k[...], v[...], g[...]
    cross = g_all.astype(F32) * mixed[...].astype(F32)
    d_left = jnp.sum(jnp.where(left, cross, 0.0), axis=1, keepdims=True)
    d_right = jnp.sum(jnp.where(left, 0.0, cross), axis=1, keepdims=True)
    q_tail = three_terms(-pltpu.roll(total[...], HDIM, 1), 4, seg_q[...])
    g_tail = three_terms(jnp.where(left, -d_right, -d_left), 0, jnp.zeros_like(g_all))
    k_tail = seg_k[...] + jnp.where((lane >= 4) & (lane < 7), 1.0, 0.0).astype(LOW)
    v_tail = jnp.broadcast_to(jnp.where(lane < 3, 1.0, 0.0).astype(LOW), v_all.shape)
    zero = jnp.zeros_like(k_all)
    dk, dv, dq_t = [], [], None
    for h in range(2):
        mine = left if h == 0 else jnp.logical_not(left)
        p = jnp.exp(dot_nt(jnp.where(mine, k_all, k_tail), jnp.where(mine, q_all, q_tail)))
        dp = dot_nt(jnp.where(mine, v_all, v_tail), jnp.where(mine, g_all, g_tail))
        ds = (p * dp).astype(LOW)
        dv.append(dot_nn(p.astype(LOW), g_all))
        dk.append(dot_nn(ds, q_all))
        part = dot_nn(jnp.where(mine, k_all, zero).astype(F32).T.astype(LOW), ds)
        dq_t = part if dq_t is None else dq_t + part
    dk = jnp.where(left, dk[0], dk[1])
    dv = jnp.where(left, dv[0], dv[1])
    dq = dq_t.T * HDIM ** (-0.5)
    dproj[0] = dq.astype(LOW)
    dproj[1] = dk.astype(LOW)
    dproj[2] = dv.astype(LOW)
    sums[0:1, :] = colsum(dq)
    sums[1:2, :] = colsum(dv)


def ff_fwd_kernel(
    meta, tok, mixed_own, mixed_oth, own0, own1, oth0, oth1, w_ff, vecs, b_up,
    norm_two_out, normed_out, inv_out, act_out, slope_out, block_out, low_out, stats,
    wo_own, wo_oth, sems_own, sems_oth,
):
    out_rows = wo_own.shape[2]
    copies = fetch(meta, (own0, own1), 3 * out_rows, out_rows, wo_own, sems_own)
    copies += fetch(meta, (oth0, oth1), 3 * out_rows, out_rows, wo_oth, sems_oth)
    in_first_step(copies, "start")
    in_first_step(copies, "wait")
    attn = (
        dot_nt(mixed_own[...], flat(wo_own[...]))
        + dot_nt(mixed_oth[...], flat(wo_oth[...]))
        + vecs[2:3]
    )
    resid = tok[...].astype(F32) + attn
    normed, inv = norm_parts(resid)
    norm_two = (normed * vecs[3:4] + vecs[4:5]).astype(LOW)
    norm_two_out[...] = norm_two
    normed_out[...] = normed.astype(LOW)
    inv_out[...] = jnp.broadcast_to(inv, inv_out.shape)
    wide = w_ff.shape[-1]
    ff = act_out.shape[-1]
    parts = ff // wide
    tall = w_ff.shape[2] // (2 * parts)
    mlp = vecs[5:6]
    before = None
    for n in range(2 * parts + 1):
        if n < 2 * parts:
            side, c = divmod(n, parts)
            at_side = meta[TP] if side == 0 else 1 - meta[TP]
            at = slice(c * wide, (c + 1) * wide)
            pre = dot_nn(norm_two, flat(w_ff[:, at_side, c * tall : (c + 1) * tall, :]))
            pre = pre + b_up[side : side + 1, at]
        if before is not None:
            act, side_b, c_b = before
            down = slice((parts + c_b) * tall, (parts + c_b + 1) * tall)
            mlp = mlp + dot_nt(act, flat(w_ff[:, side_b, down, :]))
        if n < 2 * parts:
            act, slope = gelu_parts(pre)
            act = act.astype(LOW)
            if side == 0:
                act_out[:, at] = act
            slope_out[:, side * ff + c * wide : side * ff + (c + 1) * wide] = slope.astype(LOW)
            before = (act, at_side, c)
    block = resid + mlp
    block_out[...] = block
    low_out[...] = block.astype(LOW)

    @pl.when(pl.program_id(0) == 0)
    def _():
        stats[...] = jnp.zeros_like(stats)

    valid, _ = row_masks(meta, block.shape[0])
    stats[0:1, :] += colsum(block * block * valid)
    stats[1:2, :] += colsum(attn * attn * valid)
    stats[2:3, :] += colsum(mlp * mlp * valid)


def head_kernel(
    meta, block, lat, g_block, g_head, own0, own1, oth0, oth1, b_mod, b_hid1, b_hid2,
    head_out, g_lat, hid_in_out, hidden_out, branch_low_out, pre_low_out, mod_low_out, cond_out,
    dblock_out, dblock_low_out, sums_w, sums_h, sums_d,
    w_own, w_oth, sems_own, sems_oth,
):
    copies = fetch(meta, (own0, own1), 0, w_own.shape[2], w_own, sems_own)
    copies += fetch(meta, (oth0, oth1), 0, w_oth.shape[2], w_oth, sems_oth)
    in_first_step(copies, "start")
    half = hidden_out.shape[-1]
    in_rows = 2 * half // SHARDS
    mod_rows = block.shape[-1] // SHARDS

    def hid(which, side):
        w = w_own if side == 0 else w_oth
        return flat(w[:, :, which * in_rows : (which + 1) * in_rows, :])

    def mod(t, side):
        at = 2 * in_rows + (2 * t + side) * mod_rows
        return flat(w_own[:, :, at : at + mod_rows, :])

    def modulation(t):
        parts = [dot_nn(cond, mod(t, side)) for side in range(2)]
        return jnp.concatenate(parts, axis=1) + b_mod[t : t + 1]

    valid, image = row_masks(meta, block.shape[0])
    blk = block[...]
    sig_b = sigmoid(blk)
    cond = (blk * sig_b).astype(LOW)
    cond_out[...] = cond
    lat_in = lat[...].astype(F32)
    lat_norm, lat_inv = norm_parts(lat_in)
    in_first_step(copies, "wait")
    shift = modulation(0)
    scale = 1.0 + modulation(1)
    gate = modulation(2)
    hid_in = (lat_norm * scale + shift).astype(LOW)
    hid_in_out[...] = hid_in
    branch = b_hid2[...]
    slopes = []
    for side in range(2):
        pre = dot_nn(hid_in, hid(0, side)) + b_hid1[side : side + 1]
        sig = sigmoid(pre)
        hidden = (pre * sig).astype(LOW)
        slopes.append(sig * (1.0 + pre * (1.0 - sig)))
        if side == 0:
            hidden_out[...] = hidden
        branch = branch + dot_nt(hidden, hid(1, side))
    head_branch = gate * branch
    head_out[...] = (lat_in + head_branch).astype(LOW)
    gh = g_head[...].astype(F32) * image
    dbranch = gh * gate
    branch_low = dbranch.astype(LOW)
    branch_low_out[...] = branch_low
    dgate = gh * branch

    @pl.when(pl.program_id(0) == 0)
    def _():
        sums_w[...] = jnp.zeros_like(sums_w)
        sums_h[...] = jnp.zeros_like(sums_h)
        sums_d[...] = jnp.zeros_like(sums_d)

    dhid_in = None
    for side in range(2):
        dpre = dot_nn(branch_low, hid(1, side)) * slopes[side]
        pre_low = dpre.astype(LOW)
        if side == 0:
            pre_low_out[...] = pre_low
            sums_h[0:1, :] += colsum(dpre)
        part = dot_nt(pre_low, hid(0, side))
        dhid_in = part if dhid_in is None else dhid_in + part
    dscale = dhid_in * lat_norm
    lows = [dhid_in.astype(LOW), dscale.astype(LOW), dgate.astype(LOW)]
    dcond = None
    for t in range(3):
        mod_low_out[t] = jnp.where(meta[TP] == 0, lows[t][:, :half], lows[t][:, half:])
        for side in range(2):
            part = dot_nt(lows[t][:, side * half : (side + 1) * half], mod(t, side))
            dcond = part if dcond is None else dcond + part
    sums_w[0:1, :] += colsum(dbranch)
    sums_w[1:2, :] += colsum(dhid_in)
    sums_w[2:3, :] += colsum(dscale)
    sums_w[3:4, :] += colsum(dgate)
    sums_w[4:5, :] += colsum(head_branch * head_branch * valid)
    g_lat[...] = gh + norm_back(dhid_in * scale, lat_norm, lat_inv)
    dblock = g_block[...].astype(F32) * valid + dcond * (sig_b * (1.0 + blk * (1.0 - sig_b)))
    dblock_out[...] = dblock
    dblock_low_out[...] = dblock.astype(LOW)
    sums_d[0:1, :] += colsum(dblock)


def ff_bwd_kernel(
    meta, dblock, dblock_low, slope, normed_in, inv_in, own0, own1, oth0, oth1, w_ff, vecs,
    dup_out, dresid_out, dresid_low_out, dmixed_own_out, dmixed_oth_out, sums_u, sums_d,
    wo_own, wo_oth, sems_own, sems_oth,
):
    out_rows = wo_own.shape[2]
    copies = fetch(meta, (own0, own1), 3 * out_rows, out_rows, wo_own, sems_own)
    copies += fetch(meta, (oth0, oth1), 3 * out_rows, out_rows, wo_oth, sems_oth)
    in_first_step(copies, "start")
    wide = w_ff.shape[-1]
    ff = dup_out.shape[-1]
    parts = ff // wide
    tall = w_ff.shape[2] // (2 * parts)

    @pl.when(pl.program_id(0) == 0)
    def _():
        sums_u[...] = jnp.zeros_like(sums_u)
        sums_d[...] = jnp.zeros_like(sums_d)

    low_in = dblock_low[...]
    dnorm = None
    for n in range(2 * parts):
        side, c = divmod(n, parts)
        at_side = meta[TP] if side == 0 else 1 - meta[TP]
        at = slice(c * wide, (c + 1) * wide)
        down = slice((parts + c) * tall, (parts + c + 1) * tall)
        dact = dot_nn(low_in, flat(w_ff[:, at_side, down, :]))
        dpre = dact * slope[:, side * ff + c * wide : side * ff + (c + 1) * wide].astype(F32)
        dup = dpre.astype(LOW)
        if side == 0:
            dup_out[:, at] = dup
            sums_u[0:1, at] += colsum(dpre)
        part = dot_nt(dup, flat(w_ff[:, at_side, c * tall : (c + 1) * tall, :]))
        dnorm = part if dnorm is None else dnorm + part
    normed = normed_in[...].astype(F32)
    sums_d[0:1, :] += colsum(dnorm * normed)
    sums_d[1:2, :] += colsum(dnorm)
    dresid = dblock[...] + norm_back(dnorm * vecs[3:4], normed, inv_in[:, 0:1])
    sums_d[2:3, :] += colsum(dresid)
    dresid_out[...] = dresid
    low = dresid.astype(LOW)
    dresid_low_out[...] = low
    in_first_step(copies, "wait")
    dmixed_own_out[...] = dot_nn(low, flat(wo_own[...])).astype(LOW)
    dmixed_oth_out[...] = dot_nn(low, flat(wo_oth[...])).astype(LOW)


def tok_bwd_kernel(
    meta, tok, dproj_own, dproj_oth, dresid, own0, own1, oth0, oth1, vecs, g_tok, sums,
    w_own, w_oth, sems_own, sems_oth,
):
    copies = fetch(meta, (own0, own1), 0, w_own.shape[2], w_own, sems_own)
    copies += fetch(meta, (oth0, oth1), 0, w_oth.shape[2], w_oth, sems_oth)
    in_first_step(copies, "start")
    normed, inv = norm_parts(tok[...].astype(F32))

    @pl.when(pl.program_id(0) == 0)
    def _():
        sums[...] = jnp.zeros_like(sums)

    in_first_step(copies, "wait")
    dnorm = None
    for dproj, w in ((dproj_own, w_own), (dproj_oth, w_oth)):
        rows = w.shape[2] // 3
        for t in range(3):
            part = dot_nt(dproj[t], flat(w[:, :, t * rows : (t + 1) * rows, :]))
            dnorm = part if dnorm is None else dnorm + part
    sums[0:1, :] += colsum(dnorm * normed)
    sums[1:2, :] += colsum(dnorm)
    g_tok[...] = dresid[...] + norm_back(dnorm * vecs[0:1], normed, inv)


def weight_grads(meta, products, apart):
    arrays, where = [], {}
    for left, right, _ in products:
        for arr in (left, right):
            if id(arr) not in where:
                where[id(arr)] = len(arrays)
                arrays.append(arr)
    plan, at = [], 0
    for left, right, index in products:
        rows = left.shape[1] // SHARDS
        plan.append((where[id(left)], where[id(right)], index, at, rows))
        at += rows
    total, cols = at, products[0][1].shape[-1]
    n_in, n_out = len(arrays), 2 if apart else 1

    def kernel(meta, *refs):
        ins, outs = refs[:n_in], refs[n_in : n_in + n_out]
        held, (stage, sems_in, sems_out) = refs[n_in + n_out : -3], refs[-3:]
        core = meta[CORE]
        loads = [
            pltpu.make_async_copy(ref, buf, sems_in.at[i]) for i, (ref, buf) in enumerate(zip(ins, held))
        ]
        for load in loads:
            load.start()
        waited, stores = set(), []
        for n, (left, right, index, at, rows) in enumerate(plan):
            for i in (left, right):
                if i not in waited:
                    waited.add(i)
                    loads[i].wait()
            other = held[right][...] if index is None else held[right][index]
            grad = dot_tn(held[left][...], other).astype(LOW)
            stage[:, :, at : at + rows, :] = grad.reshape(SHARDS // 2, 2, rows, cols)
            for i, out in enumerate(outs):
                frm, to = stage.at[:, :, at : at + rows, :], out.at[..., at : at + rows, :]
                if apart:
                    frm = stage.at[:, core if i == 0 else 1 - core, at : at + rows, :]
                store = pltpu.make_async_copy(frm, to, sems_out.at[n_out * n + i])
                store.start()
                stores.append(store)
        for store in stores:
            store.wait()

    shape = sds((SHARDS // 2, *(() if apart else (2,)), total, cols), LOW)
    macs = sum(left.shape[0] * left.shape[1] * cols for left, _, _ in products)
    return run(
        kernel, meta, 1,
        [(arr, ANY) for arr in arrays],
        [(shape, ANY)] * n_out,
        scratch=[pltpu.VMEM(arr.shape, LOW) for arr in arrays]
        + [
            pltpu.VMEM((SHARDS // 2, 2, total, cols), LOW),
            pltpu.SemaphoreType.DMA((n_in,)),
            pltpu.SemaphoreType.DMA((n_out * len(plan),)),
        ],
        flops=2 * macs,
        nbytes=4 * SHARDS * total * cols,
    )


SWAP = [(0, 1), (1, 0)]
SWAP_CORE = [(i, i ^ 1) for i in range(SHARDS)]
SWAP_Y = [(i, i ^ 2) for i in range(SHARDS)]
hold = lax.optimization_barrier


def shift_z(step):
    return [(z * 4 + r, ((z + step) % 4) * 4 + r) for z in range(4) for r in range(4)]


def place(n_dp):
    if n_dp != SHARDS:
        zero = jnp.zeros((), jnp.int32)
        return zero, zero, zero
    at = lax.axis_index("dp")
    return at // 4, (at // 2) % 2, at % 2


def pick(arr, i, axis):
    return lax.dynamic_index_in_dim(arr, i, axis, keepdims=False)


def regroup(full):
    n_dp = full.shape[0]
    per = n_dp // SHARDS
    mid = full.shape[1:-2]
    split = full.reshape(SHARDS, per, *mid, *full.shape[-2:])
    order = (0, *range(2, 2 + len(mid)), 1, 2 + len(mid), 3 + len(mid))
    return jnp.transpose(split, order).reshape(SHARDS, *mid, per * full.shape[-2], full.shape[-1])


def by_core(full):
    _, n, rows, cols = full.shape
    split = full.reshape(SHARDS // 2, 2, n * rows, cols)
    return split[:, 0], split[:, 1]


def gather_both(group, n_dp):
    full = lax.all_gather(group, ("dp", "tp"), axis=0).reshape(n_dp, 2, *group.shape)
    full = regroup(full)
    tp = lax.axis_index("tp")
    return pick(full, tp, 1), pick(full, 1 - tp, 1)


class Gather:
    def __init__(self, block, where):
        self.block, (self.z, self.y, _) = block, where
        self.from_y = lax.ppermute(block, "dp", SWAP_Y)
        self.along_z = [lax.ppermute(block, "dp", shift_z(s)) for s in (1, 2, 3)]

    def cross_y(self):
        self.rest = lax.ppermute(jnp.stack(self.along_z), "dp", SWAP_Y)

    def finish(self):
        buf = jnp.zeros((4, 2, *self.block.shape), LOW)
        zero = jnp.zeros((), jnp.int32)
        for s in range(4):
            at = (self.z - s) % 4
            mine = self.block if s == 0 else self.along_z[s - 1]
            theirs = self.from_y if s == 0 else self.rest[s - 1]
            for piece, y in ((mine, self.y), (theirs, 1 - self.y)):
                buf = lax.dynamic_update_slice(buf, piece[None, None], (at, y, zero, zero))
        return buf.reshape(8, *self.block.shape)


def swap_core(block):
    return lax.ppermute(block, "dp", SWAP_CORE)


def gather_ff(w_up, w_down, wide, n_dp):
    cols = lambda w: jnp.transpose(w.reshape(w.shape[0], -1, wide), (1, 0, 2))
    parts = jnp.concatenate([cols(w_up), cols(w_down)])
    full = lax.all_gather(parts, ("dp", "tp"), axis=0).reshape(n_dp, 2, *parts.shape)
    return regroup(full).reshape(SHARDS, 2, -1, wide)


def pack_head(w_hid1, w_hid2, w_mod):
    t, rows, cols = w_mod.shape
    wide = w_hid1.shape[1]
    mod = jnp.transpose(w_mod.reshape(t, rows, cols // wide, wide), (0, 2, 1, 3))
    return jnp.stack([w_hid1, w_hid2]), mod.reshape(-1, rows, wide)


class Scatter:
    def __init__(self, here, there, where):
        self.z, self.y, _ = where
        part = (here.astype(F32) + swap_core(there).astype(F32)).astype(LOW)
        self.part = part.reshape(4, 2, *here.shape[1:])

    def start_y(self):
        self.got = lax.ppermute(pick(self.part, 1 - self.y, 1), "dp", SWAP_Y)

    def add_y(self):
        self.part = (pick(self.part, self.y, 1).astype(F32) + self.got.astype(F32)).astype(LOW)

    def start_z(self):
        self.got = [
            lax.ppermute(pick(self.part, (self.z + s) % 4, 0), "dp", shift_z(s)) for s in (1, 2, 3)
        ]

    def result(self):
        total = pick(self.part, self.z, 0).astype(F32)
        for got in self.got:
            total = total + got.astype(F32)
        return total


class ScatterAny:
    def __init__(self, here, there, rows, n_dp):
        self.total = scatter_whole(jnp.stack([here, there], axis=1), rows, n_dp)
        self.part = self.got = jnp.zeros((), LOW)

    def start_y(self):
        pass

    add_y = start_z = start_y

    def result(self):
        return self.total


def scatter_whole(packed, rows, n_dp):
    packed = packed.reshape(SHARDS, *packed.shape[2:])
    per = n_dp // SHARDS
    if per > 1:
        parts, at = [], 0
        for r in rows:
            part = packed[:, at : at + r]
            parts.append(part.reshape(n_dp, r // per, packed.shape[-1]))
            at += r
        packed = jnp.concatenate(parts, axis=1)
    return lax.psum_scatter(packed, "dp", scatter_dimension=0, tiled=False).astype(F32)


def sum_all(vector, n_dp):
    if n_dp != SHARDS:
        return lax.psum(vector, "dp")
    for swap in (SWAP_CORE, SWAP_Y, [(i, i ^ 4) for i in range(16)], [(i, i ^ 8) for i in range(16)]):
        vector = vector + lax.ppermute(vector, "dp", swap)
    return vector


def on_device(
    tokens, latents, grad_block, grad_head, image_lengths, ln1_gain, ln1_bias, w_qkv, b_qv, w_out,
    b_out, ln2_gain, ln2_bias, w_up, b_up, w_down, b_down, w_mod, b_mod, w_hid1, b_hid1, w_hid2,
    b_hid2,
):
    rows, width = tokens.shape
    head_width = latents.shape[1]
    half = w_qkv.shape[2]
    ff = w_up.shape[1]
    hid = w_hid1.shape[1]
    n_dp = width // w_out.shape[0]
    direct = n_dp == SHARDS
    tp = lax.axis_index("tp")
    where = place(n_dp)
    core = where[2]
    pairs = half // 128
    tall, short = rows // 2, rows // 4
    out_rows, in_rows = width // SHARDS, head_width // SHARDS

    early = jnp.concatenate([w_qkv.reshape(-1, half), w_out])
    hid_part, mod_part = pack_head(w_hid1, w_hid2, w_mod)
    if direct:
        gather_one = Gather(early, where)
        gather_one.cross_y()
        own_first = gather_one.finish()
        early_own = (own_first, swap_core(own_first))
        across = lax.ppermute(own_first, "tp", SWAP)
        late = jnp.concatenate([hid_part.reshape(-1, hid), mod_part.reshape(-1, hid)])
        late, _ = hold((late, gather_one.along_z))
        gather_two = Gather(late, where)
    else:
        got = gather_both(jnp.concatenate([w_qkv, w_out[None]]), n_dp)
        early_own, early_oth = by_core(got[0]), by_core(got[1])
        hid_own, hid_oth = gather_both(hid_part, n_dp)
        mod_all = regroup(lax.all_gather(mod_part, "dp", axis=0))
        late_own = tuple(
            jnp.concatenate([h, m], axis=1) for h, m in zip(by_core(hid_own), by_core(mod_all))
        )
        late_oth = by_core(hid_oth)
    w_ff = gather_ff(w_up, w_down, hid, n_dp)

    mine = jnp.concatenate([b_qv.reshape(-1), b_up, b_hid1])
    theirs = lax.ppermute(mine, "tp", SWAP)
    cut = lambda v: (v[: 2 * half].reshape(2, half), v[2 * half : 2 * half + ff], v[2 * half + ff :])
    (bqv_own, bup_own, bhid_own), (bqv_oth, bup_oth, bhid_oth) = cut(mine), cut(theirs)
    b_up2 = jnp.stack([bup_own, bup_oth])
    b_hid2x = jnp.stack([bhid_own, bhid_oth])
    vecs = jnp.stack([ln1_gain, ln1_bias, b_out, ln2_gain, ln2_bias, b_down])
    last_bias = b_hid2.reshape(1, -1)

    ends = jnp.cumsum(image_lengths[0])
    meta = jnp.concatenate([tp.reshape(1), core.reshape(1), ends]).astype(jnp.int32)
    at = jnp.arange(rows, dtype=jnp.int32)[:, None]
    segment = jnp.sum((at >= ends[None, :]).astype(jnp.int32), axis=1, keepdims=True)
    lane_of = (jnp.arange(128) % HDIM)[None, :]
    same = segment == lane_of
    seg_q = jnp.where(same & (lane_of < 4), 1.0, 0.0).astype(LOW)
    seg_k = jnp.where(jnp.logical_not(same) & (lane_of < 4), FAR, 0.0).astype(LOW)

    tall3 = pl.BlockSpec((3, tall, half), lambda i, meta: (0, i, 0))
    keep = lambda n, w: (sds((n, w), F32), sum_spec(n, w))
    pair_spec = pl.BlockSpec((rows, 128), lambda p, meta: (0, p))
    whole = pl.BlockSpec((rows, 128), lambda p, meta: (0, 0))
    part_spec = lambda t: pl.BlockSpec((None, rows, 128), lambda p, meta: (t, 0, p))
    proj_shape = (sds((3, rows, half), LOW), tall3)
    attn_cost = rows * rows * 256 * 2 * pairs
    vec_in = (vecs, const_spec(*vecs.shape))
    pair_in = lambda pair: [(pair[0], ANY), (pair[1], ANY)]
    pair_buf = lambda n, cols: pltpu.VMEM((SHARDS // 2, 2, n, cols), LOW)
    two_sems = pltpu.SemaphoreType.DMA((2,))

    def attend(proj):
        return run(
            attn_fwd_kernel, meta, pairs,
            [
                (proj, part_spec(0)), (proj, part_spec(1)), (proj, part_spec(2)),
                (seg_q, whole), (seg_k, whole),
            ],
            [(sds((rows, half), LOW), pair_spec), (sds((rows, half), F32), pair_spec)],
            flops=4 * attn_cost,
            nbytes=12 * rows * half,
            exps=2 * pairs * rows * rows,
        )

    def attend_back(proj, dmixed, mixed, total):
        return run(
            attn_bwd_kernel, meta, pairs,
            [
                (proj, part_spec(0)), (proj, part_spec(1)), (proj, part_spec(2)),
                (dmixed, pair_spec), (mixed, pair_spec), (total, pair_spec),
                (seg_q, whole), (seg_k, whole),
            ],
            [
                (sds((3, rows, half), LOW), pl.BlockSpec((3, rows, 128), lambda p, meta: (0, 0, p))),
                (sds((8, half), F32), pl.BlockSpec((8, 128), lambda p, meta: (0, p))),
            ],
            flops=10 * attn_cost,
            nbytes=20 * rows * half,
            exps=2 * pairs * rows * rows,
        )

    norm_one, proj_own = run(
        qkv_own_kernel, meta, 2,
        [
            (tokens, row_spec(tall, width)), vec_in, *pair_in(early_own),
            (bqv_own, const_spec(2, half)),
        ],
        [(sds((rows, width), LOW), row_spec(tall, width)), proj_shape],
        scratch=[pair_buf(3 * out_rows, half), two_sems],
        flops=6 * rows * width * half,
        nbytes=10 * rows * width,
    )
    if direct:
        across, proj_own = hold((across, proj_own))
    mixed_own, total_own = attend(proj_own)
    if direct:
        early_oth = (across, swap_core(across))
        gather_two.along_z, mixed_own = hold((gather_two.along_z, mixed_own))
        gather_two.cross_y()
    (proj_oth,) = run(
        qkv_other_kernel, meta, 2,
        [
            (norm_one, row_spec(tall, width)), *pair_in(early_oth),
            (bqv_oth, const_spec(2, half)),
        ],
        [proj_shape],
        scratch=[pair_buf(3 * out_rows, half), two_sems],
        flops=6 * rows * width * half,
        nbytes=8 * rows * width,
    )
    mixed_oth, total_oth = attend(proj_oth)
    if direct:
        gather_two.rest, mixed_oth = hold((gather_two.rest, mixed_oth))
        late_first = gather_two.finish()
        late_own = (late_first, swap_core(late_first))
        late_across = lax.ppermute(late_first[:, : 2 * in_rows], "tp", SWAP)

    early_in = pair_in(early_own) + pair_in(early_oth)
    ff_block = const_spec(*w_ff.shape)
    norm_two, normed_two, inv_two, act, slope, block, block_low, stats = run(
        ff_fwd_kernel, meta, 4,
        [
            (tokens, row_spec(short, width)), (mixed_own, row_spec(short, half)),
            (mixed_oth, row_spec(short, half)), *early_in, (w_ff, ff_block), vec_in,
            (b_up2, const_spec(2, ff)),
        ],
        [
            (sds((rows, width), LOW), row_spec(short, width)),
            (sds((rows, width), LOW), row_spec(short, width)),
            (sds((rows, 128), F32), row_spec(short, 128)),
            (sds((rows, ff), LOW), row_spec(short, ff)),
            (sds((rows, 2 * ff), LOW), row_spec(short, 2 * ff)),
            (sds((rows, width), F32), row_spec(short, width)),
            (sds((rows, width), LOW), row_spec(short, width)),
            keep(8, width),
        ],
        scratch=[pair_buf(out_rows, half), pair_buf(out_rows, half), two_sems, two_sems],
        flops=2 * rows * width * (4 * ff + width),
        nbytes=rows * (20 * width + 6 * ff) + 8 * width * ff,
        exps=4 * rows * ff,
    )
    if direct:
        late_across, block = hold((late_across, block))
        late_oth = (late_across, swap_core(late_across))

    (
        head_out, grad_latents, hid_in, hidden, branch_low, pre_low, mod_low, cond, dblock,
        dblock_low, sums_w, sums_h, sums_b,
    ) = run(
        head_kernel, meta, 4,
        [
            (block, row_spec(short, width)), (latents, row_spec(short, head_width)),
            (grad_block, row_spec(short, width)), (grad_head, row_spec(short, head_width)),
            *pair_in(late_own), *pair_in(late_oth),
            (b_mod, const_spec(3, head_width)), (b_hid2x, const_spec(2, hid)),
            (last_bias, const_spec(1, head_width)),
        ],
        [
            (sds((rows, head_width), LOW), row_spec(short, head_width)),
            (sds((rows, head_width), F32), row_spec(short, head_width)),
            (sds((rows, head_width), LOW), row_spec(short, head_width)),
            (sds((rows, hid), LOW), row_spec(short, hid)),
            (sds((rows, head_width), LOW), row_spec(short, head_width)),
            (sds((rows, hid), LOW), row_spec(short, hid)),
            (sds((3, rows, hid), LOW), pl.BlockSpec((3, short, hid), lambda i, meta: (0, i, 0))),
            (sds((rows, width), LOW), row_spec(short, width)),
            (sds((rows, width), F32), row_spec(short, width)),
            (sds((rows, width), LOW), row_spec(short, width)),
            keep(8, head_width), keep(8, hid), keep(8, width),
        ],
        scratch=[
            pair_buf(late_own[0].shape[1], hid), pair_buf(2 * in_rows, hid), two_sems, two_sems,
        ],
        flops=2 * rows * head_width * (6 * width + 4 * head_width),
        nbytes=rows * (14 * width + 22 * head_width) + 20 * head_width * head_width,
        exps=rows * 2 * head_width,
    )

    def scatter(products):
        here, there = weight_grads(meta, products, True)
        if direct:
            return Scatter(here, there, where)
        return ScatterAny(here, there, [p[0].shape[1] // SHARDS for p in products], n_dp)

    products = [
        (hid_in, pre_low, None), (branch_low, hidden, None), (cond, mod_low, 0),
        (cond, mod_low, 1), (cond, mod_low, 2),
    ]
    (packed,) = weight_grads(meta, products, False)
    packed, dblock_low = hold((packed, dblock_low))
    got_head = scatter_whole(packed, [p[0].shape[1] // SHARDS for p in products], n_dp)
    down = scatter([(dblock_low, act, None)])
    down.part, dblock = hold((down.part, dblock))
    down.start_y()

    dup, dresid, dresid_low, dmixed_own, dmixed_oth, sums_u, sums_r = run(
        ff_bwd_kernel, meta, 2,
        [
            (dblock, row_spec(tall, width)), (dblock_low, row_spec(tall, width)),
            (slope, row_spec(tall, 2 * ff)), (normed_two, row_spec(tall, width)),
            (inv_two, row_spec(tall, 128)), *early_in, (w_ff, ff_block), vec_in,
        ],
        [
            (sds((rows, ff), LOW), row_spec(tall, ff)),
            (sds((rows, width), F32), row_spec(tall, width)),
            (sds((rows, width), LOW), row_spec(tall, width)),
            (sds((rows, half), LOW), row_spec(tall, half)),
            (sds((rows, half), LOW), row_spec(tall, half)),
            keep(8, ff), keep(8, width),
        ],
        scratch=[pair_buf(out_rows, half), pair_buf(out_rows, half), two_sems, two_sems],
        flops=2 * rows * width * (4 * ff + width),
        nbytes=rows * (16 * width + 6 * ff) + 8 * width * ff,
    )
    up = scatter([(norm_two, dup, None)])
    down.got, up.part, dmixed_own = hold((down.got, up.part, dmixed_own))
    down.add_y()
    down.part, up.part, dmixed_own = hold((down.part, up.part, dmixed_own))
    down.start_z()
    up.start_y()

    dproj_own, sums_qv = attend_back(proj_own, dmixed_own, mixed_own, total_own)
    down.got, up.got, dproj_own = hold((down.got, up.got, dproj_own))
    up.add_y()
    up.part, dproj_own = hold((up.part, dproj_own))
    up.start_z()
    attn = scatter(
        [(norm_one, dproj_own, 0), (norm_one, dproj_own, 1), (norm_one, dproj_own, 2), (dresid_low, mixed_own, None)]
    )
    attn.part, dmixed_oth = hold((attn.part, dmixed_oth))
    attn.start_y()
    dproj_oth, _ = attend_back(proj_oth, dmixed_oth, mixed_oth, total_oth)
    up.got, attn.got, got_head, dproj_oth = hold((up.got, attn.got, got_head, dproj_oth))
    attn.add_y()
    attn.part, dproj_oth = hold((attn.part, dproj_oth))
    attn.start_z()
    w_rows, w_in = width // n_dp, head_width // n_dp
    mod_mine = got_head[2 * w_in :].reshape(3, -1, hid)
    mod_theirs = lax.ppermute(mod_mine, "tp", SWAP)
    grad_tokens, sums_t = run(
        tok_bwd_kernel, meta, 2,
        [
            (tokens, row_spec(tall, width)), (dproj_own, tall3), (dproj_oth, tall3),
            (dresid, row_spec(tall, width)), *early_in, vec_in,
        ],
        [(sds((rows, width), F32), row_spec(tall, width)), keep(8, width)],
        scratch=[pair_buf(3 * out_rows, half), pair_buf(3 * out_rows, half), two_sems, two_sems],
        flops=2 * rows * width * 3 * width,
        nbytes=16 * rows * width,
    )

    pieces = [
        sums_t[0:2].reshape(-1), sums_qv[0:2].reshape(-1), sums_r[0:3].reshape(-1),
        sums_u[0], sums_b[0], sums_w[0:4].reshape(-1), sums_h[0],
    ]
    sizes = [p.shape[0] for p in pieces]
    joined = jnp.concatenate(pieces)
    joined = jnp.pad(joined, (0, -joined.shape[0] % 1024)).reshape(-1, 128)
    summed = sum_all(joined, n_dp).reshape(-1)
    split, begin = [], 0
    for size in sizes:
        split.append(summed[begin : begin + size])
        begin += size
    ln1s, bqv, rs, d_b_up, d_b_down, ws, d_b_hid1 = split
    ln1s, bqv, rs = ln1s.reshape(2, -1), bqv.reshape(2, -1), rs.reshape(3, -1)
    ws = ws.reshape(4, -1)

    d_w_hid1, d_w_hid2 = got_head[:w_in], got_head[w_in : 2 * w_in]
    first = tp == 0
    d_w_mod = jnp.concatenate(
        [jnp.where(first, mod_mine, mod_theirs), jnp.where(first, mod_theirs, mod_mine)], axis=2
    )
    got = attn.result()
    d_w_qkv = got[: 3 * w_rows].reshape(3, w_rows, half)
    d_w_out = got[3 * w_rows :]

    squares = jnp.concatenate([jnp.sum(stats[0:3], axis=1), jnp.sum(sums_w[4:5], axis=1)])
    widths = jnp.array([width, width, width, head_width], F32)
    count = jnp.clip(ends[2], 0, rows).astype(F32)
    rms_values = jnp.sqrt(squares / (count * widths)).reshape(1, 4)
    return (
        block_low, head_out, grad_tokens, grad_latents, ln1s[0], ln1s[1], d_w_qkv, bqv, d_w_out,
        rs[2], rs[0], rs[1], up.result(), d_b_up, down.result(), d_b_down, d_w_mod, ws[1:4], d_w_hid1,
        d_b_hid1, d_w_hid2, ws[0], rms_values,
    )


def solution(mesh):
    rows, one = P("dp", None), P()
    split = P("dp", "tp")
    weights = (
        one, one, P(None, "dp", "tp"), P(None, "tp"), split, one, one, one, split, P("tp"), split,
        one, P(None, "dp", None), one, split, P("tp"), split, one,
    )
    return jax.shard_map(
        on_device,
        mesh=mesh,
        in_specs=(rows, rows, rows, rows, rows) + weights,
        out_specs=(rows, rows, rows, rows) + weights + (rows,),
        check_vma=False,
    )
```
